32 devices in a mesh: quad: 4 (over z), row: 8 (over y, x, core).
Axes of the slice: x: 2, y: 2, z: 4, core: 2. Of those that a mesh axis runs over, the one named last changes fastest.
Arguments:
- hamiltonian: bfloat16 [512, 64, 1536], P('row'), may hold values from -0.15625 to 0.15625
- columns: int32 [512, 24], P('row'), may hold values from 0 to 511, as said below
- counts: int32 [512], P('row'), may hold values from 2 to 24, as said below
- precond: bfloat16 [8, 512, 64, 128], P('quad', 'row'), may hold values from -0.5 to 0.5
- rhs: bfloat16 [32768, 128], P('row'), may hold values from -6 to 6
Outputs:
- moments_out: float32 [8, 32768, 128], P('quad', 'row')
- blocks_out: float32 [8, 128, 128], P('quad')
The draws below stay inside these ranges and needn't reach their ends.
Inputs may be any that keep to these rules, and one draw needn't show every extreme that they name: `columns`: slot 0 of row block b holds b itself; slot 1 holds b - 64 for even b and b + 64 for odd b, reflected at the ends (an index -m becomes m, an index 511 + m becomes 512 - 1 - m); every column block lies within 64 blocks of its row block. `counts`: every run of 64 row blocks starting at a multiple of 64 holds a row block with all 24 slots live.
All inputs are finite; a program needn't handle non-finite values.
Results may differ from the reference program's by a relative error of at most 0.02.
Values may be sent and summed in bfloat16 or wider, within the bound.
A program may use at most 128 MiB of HBM per device.

```python
import math
import jax
import jax.numpy as jnp
from jax import lax

BS = 64
K = 24
COLS = 128
RB_DEV = 64
Q_DEV = 2
ITERS = 2
MOMENTS = 8
REACH = 64
NB = 512
NR = 32768
QUADS = 8
N_QUAD = 4
N_ROW = 8


def draw_columns(key, part):
    first_key = jax.random.fold_in(key, 11)
    second_key = jax.random.fold_in(key, 12)
    blocks = jnp.arange(NB, dtype=jnp.int32)[:, None]
    offsets = jax.random.randint(first_key, (NB, K), -REACH, REACH + 1, dtype=jnp.int32)
    signs = jnp.where(jax.random.randint(second_key, (NB, 1), 0, 2, dtype=jnp.int32) == 0, -1, 1)
    slot_ids = jnp.arange(K, dtype=jnp.int32)[None, :]
    forced = 1 + jnp.arange(NB, dtype=jnp.int32) % (K - 1)
    offsets = jnp.where(slot_ids == forced[:, None], signs * REACH, offsets)
    alternate = jnp.where(blocks % 2 == 0, -REACH, REACH)
    offsets = jnp.where(slot_ids == 1, alternate, offsets)
    offsets = jnp.where(slot_ids == 0, 0, offsets)
    target = jnp.abs(blocks + offsets)
    target = jnp.where(target > NB - 1, 2 * (NB - 1) - target, target)
    return target.astype(jnp.int32)


def draw_counts(key, part):
    first_key = jax.random.fold_in(key, 21)
    second_key = jax.random.fold_in(key, 22)
    values = jax.random.randint(first_key, (NB,), 2, K + 1, dtype=jnp.int32)
    position = jax.random.randint(second_key, (), 0, RB_DEV, dtype=jnp.int32)
    blocks = jnp.arange(NB, dtype=jnp.int32)
    return jnp.where(blocks % RB_DEV == position, K, values).astype(jnp.int32)


def shard_levels(own_key, shape, cuts, least, high):
    gain, own = 1.0, jax.random.fold_in(own_key, 6)
    for dim, blocks in cuts:
        heights = jnp.exp(jax.random.uniform(jax.random.fold_in(own, dim), (blocks,), jnp.float32, least / len(cuts), high / len(cuts)))
        gain = gain * jnp.repeat(heights, shape[dim] // blocks).reshape([-1 if axis == dim else 1 for axis in range(len(shape))])
    return gain


def noise(key, shape, scale, reach, split=(), kind=jnp.bfloat16):
    values = scale * jax.random.normal(key, shape, jnp.float32)
    if split:
        values = values * shard_levels(key, shape, split, -0.22, 0.18)
    return jnp.clip(values, -reach, reach).astype(kind)


def setup_inputs(seed: int = 0) -> dict:
    arg_keys = jax.random.split(jax.random.key(seed), 6)
    hamiltonian = noise(arg_keys[0], (NB, BS, K * BS), (K * BS) ** -0.5, 0.15625, ((0, 8),))
    columns = draw_columns(jax.random.fold_in(arg_keys[5], 71), 0)
    counts = draw_counts(jax.random.fold_in(arg_keys[5], 71), 0)
    precond = noise(arg_keys[3], (QUADS, NB, BS, 2 * BS), (2 * BS) ** -0.5, 0.5, ((0, 4), (1, 8)))
    rhs = noise(arg_keys[4], (NR, COLS), 1.0, 6.0, ((0, 8),))
    return {"hamiltonian": hamiltonian, "columns": columns, "counts": counts, "precond": precond, "rhs": rhs}


def rotate(values):
    half_cols = values.shape[-1] // 2
    return jnp.concatenate([-values[..., half_cols:], values[..., :half_cols]], axis=-1)

def apply_inverse(blocks_pre, resid):
    pre_float = blocks_pre.astype(jnp.float32)
    res_float = resid.astype(jnp.float32)
    stacked = jnp.concatenate([res_float, rotate(res_float)], axis=1)
    return jnp.einsum('bij,bjc->bic', pre_float, stacked)

def multiply(hamiltonian, index_table, iterate):
    padded = jnp.concatenate([iterate, jnp.zeros((1, BS, COLS), iterate.dtype)], axis=0)
    ham_groups = hamiltonian.reshape(N_ROW, RB_DEV, BS, K * BS)
    idx_groups = index_table.reshape(N_ROW, RB_DEV, K)

    def one_group(pair):
        ham_block, idx_block = pair
        gathered = padded[idx_block].astype(jnp.float32).reshape(RB_DEV, K * BS, COLS)
        return jnp.einsum('bij,bjc->bic', ham_block.astype(jnp.float32), gathered)
    return lax.map(one_group, (ham_groups, idx_groups)).reshape(NB, BS, COLS)

def reference(hamiltonian, columns, counts, precond, rhs):
    live = jnp.arange(K)[None, :] < counts[:, None]
    index_table = jnp.where(live, columns, NB).astype(jnp.int32)
    rhs_blocks = rhs.reshape(NB, BS, COLS)
    rhs_float = rhs_blocks.astype(jnp.float32)

    def solve_point(pair):
        point, blocks_pre = pair
        theta = 2.0 * jnp.pi * (point.astype(jnp.float32) + 0.5) / QUADS
        zreal = jnp.cos(theta)
        zimag = jnp.sin(theta)
        iterate = apply_inverse(blocks_pre, rhs_blocks).astype(jnp.bfloat16)
        for sweep in range(ITERS):
            product = multiply(hamiltonian, index_table, iterate)
            current = iterate.astype(jnp.float32)
            shifted = zreal * current + zimag * rotate(current)
            resid = (rhs_float - (shifted - product)).astype(jnp.bfloat16)
            iterate = (current + apply_inverse(blocks_pre, resid)).astype(jnp.bfloat16)
        return iterate
    solutions = lax.map(solve_point, (jnp.arange(QUADS, dtype=jnp.int32), precond))
    scale = 1.0 / math.sqrt(NR)
    flat_rhs = rhs.astype(jnp.float32)
    moment_list = []
    block_list = []
    for moment in range(MOMENTS):
        total = jnp.zeros((NB, BS, COLS), jnp.float32)
        for group in range(N_QUAD):
            part = jnp.zeros((NB, BS, COLS), jnp.float32)
            for inner in range(Q_DEV):
                point = group * Q_DEV + inner
                theta = 2.0 * math.pi * (point + 0.5) / QUADS
                coef_a = math.cos((moment + 1) * theta) / QUADS
                coef_b = math.sin((moment + 1) * theta) / QUADS
                current = solutions[point].astype(jnp.float32)
                part = part + coef_a * current + coef_b * rotate(current)
            held = lax.optimization_barrier(part.astype(jnp.bfloat16))
            total = total + held.astype(jnp.float32)
        flat_total = total.reshape(NR, COLS)
        moment_list.append(flat_total)
        block_list.append(jnp.dot(flat_rhs.T, flat_total, precision=lax.Precision.HIGHEST) * scale)
    return (jnp.stack(moment_list), jnp.stack(block_list))
```

```python
import functools
import math

import jax
import jax.numpy as jnp
from jax import lax
from jax.experimental import pallas as pl
from jax.experimental.pallas import tpu as pltpu
from jax.sharding import PartitionSpec as P

ITERS = 2
MOMENTS = 8
CHUNKS = 2
TILE = 8
VMEM_LIMIT = 48 * 1024 * 1024
F32 = jnp.float32
BF16 = jnp.bfloat16


def rotated(values, h):
    width = values.shape[1]
    lane = lax.broadcasted_iota(jnp.int32, values.shape, 1)
    first = (lane // h) % 2 == 0
    ahead = pltpu.roll(values, width - h, 1)
    behind = pltpu.roll(values, h, 1)
    return jnp.where(first, -ahead, behind)


def apply_inverse(pre_ref, t, resid, h):
    per_quad = pre_ref.shape[0]
    bs, width = resid.shape
    stacked = jnp.concatenate([resid.astype(BF16), rotated(resid, h).astype(BF16)], axis=0)
    blocks = jnp.concatenate([pre_ref[q, t] for q in range(per_quad)], axis=0)
    both = jnp.dot(blocks, stacked, preferred_element_type=F32)
    lane = lax.broadcasted_iota(jnp.int32, resid.shape, 1)
    out = both[:bs]
    for q in range(1, per_quad):
        out = jnp.where(lane // (2 * h) == q, both[q * bs : (q + 1) * bs], out)
    return out


def init_kernel(h, pre_ref, rhs_ref, out_ref):
    tile, bs = out_ref.shape[0], out_ref.shape[1]
    for t in range(tile):
        out_ref[t] = apply_inverse(pre_ref, t, rhs_ref[t].astype(F32), h).astype(BF16)


def sweep_kernel(
    h, last, index_ref, ham_ref, pre_ref, rhs_ref, full_ref, coef_ref, before_ref, own_ref, after_ref, *rest
):
    if last:
        out_ref, terms_ref, held, sems = rest
    else:
        out_ref, held, sems = rest
    tile, bs, width = out_ref.shape
    nb = own_ref.shape[0]
    slots = ham_ref.shape[2] // bs
    step = pl.program_id(0)

    @pl.when(step == 0)
    def _():
        copies = [
            pltpu.make_async_copy(src, held.at[pl.ds(k * nb, nb)], sems.at[k])
            for k, src in enumerate((before_ref, own_ref, after_ref))
        ]
        for copy in copies:
            copy.start()
        held[3 * nb] = jnp.zeros((bs, width), BF16)
        if last:
            terms_ref[...] = jnp.zeros_like(terms_ref)
        for copy in copies:
            copy.wait()

    zreal = coef_ref[0:1, :]
    zimag = coef_ref[1:2, :]
    group = max(1, 256 // bs)
    for t in range(tile):
        b = step * tile + t
        product = None
        for s in range(0, slots, group):
            wide = min(group, slots - s)
            gathered = jnp.concatenate([held[index_ref[b, s + k]] for k in range(wide)], axis=0)
            term = jnp.dot(
                ham_ref[t, :, s * bs : (s + wide) * bs], gathered, preferred_element_type=F32
            )
            product = term if product is None else product + term
        current = held[nb + b].astype(F32)
        shifted = zreal * current + zimag * rotated(current, h)
        resid = (rhs_ref[t].astype(F32) - (shifted - product)).astype(BF16).astype(F32)
        out_ref[t] = (current + apply_inverse(pre_ref, t, resid, h)).astype(BF16)
    if last:
        terms_ref[...] += lax.dot_general(
            full_ref[...].reshape(tile * bs, full_ref.shape[2]),
            out_ref[...].reshape(tile * bs, width),
            (((0,), (0,)), ((), ())),
            preferred_element_type=F32,
        )


def mix_kernel(own_ref, pair_ref, mix_ref, out_ref):
    pack = jnp.concatenate([own_ref[...], pair_ref[...]], axis=1)
    wide = jnp.dot(pack, mix_ref[0], preferred_element_type=F32)
    out_ref[...] = (wide + jnp.dot(pack, mix_ref[1], preferred_element_type=F32)).astype(BF16)


def final_kernel(chunks, others, per_device, *refs):
    own, pair = refs[:chunks], refs[chunks : 2 * chunks]
    got = refs[2 * chunks : (2 + others) * chunks]
    mix_ref, place_ref, out_ref = refs[(2 + others) * chunks :]
    total = None
    for c in range(chunks):
        pack = jnp.concatenate([own[c][...], pair[c][...]], axis=1)
        part = jnp.dot(pack, mix_ref[c, 0], preferred_element_type=F32)
        part = part + jnp.dot(pack, mix_ref[c, 1], preferred_element_type=F32)
        for k in range(others):
            part = part + jnp.dot(
                got[c * others + k][...], place_ref[c], preferred_element_type=F32
            )
        total = part if total is None else total + part
    width = total.shape[1] // per_device
    for a in range(per_device):
        out_ref[a] = total[:, a * width : (a + 1) * width]


def split_two(values):
    high = values.astype(BF16)
    low = (values - high.astype(F32)).astype(BF16)
    return jnp.stack([high, low])


def shards(hamiltonian, columns, counts, precond, rhs):
    nb, bs, _ = hamiltonian.shape
    slots = columns.shape[1]
    width = rhs.shape[1]
    half = width // 2
    per_quad = precond.shape[0]
    quad_count = lax.axis_size("quad")
    row_count = lax.axis_size("row")
    quads_total = per_quad * quad_count
    per_device = MOMENTS // quad_count
    rows = nb * bs
    row_index = lax.axis_index("row")
    quad_index = lax.axis_index("quad")
    h = half // CHUNKS
    wide = per_quad * 2 * h
    tile = TILE
    params = pltpu.CompilerParams(vmem_limit_bytes=VMEM_LIMIT)

    first_block = (row_index - 1) * nb
    live = jnp.arange(slots)[None, :] < counts[:, None]
    index = jnp.where(live, columns - first_block, 3 * nb).astype(jnp.int32)

    def theta_of(j):
        return 2.0 * jnp.pi * (j.astype(F32) + 0.5) / quads_total

    points = quad_index * per_quad + jnp.arange(per_quad)
    lane_theta = jnp.repeat(theta_of(points), 2 * h)
    coefs = jnp.concatenate(
        [jnp.cos(lane_theta)[None], jnp.sin(lane_theta)[None], jnp.zeros((6, wide), F32)], axis=0
    )

    partner = quad_index + 1 - 2 * (quad_index % 2)
    pairs = quad_count // 2
    my_pair, my_side = quad_index // 2, quad_index % 2
    owners = [quad_index] + [
        ((my_pair + d) % pairs) * 2 + (1 - my_side) for d in range(1, pairs)
    ]
    moment_of = jnp.stack(owners)[:, None] * per_device + jnp.arange(per_device)[None, :]
    sources = jnp.stack([quad_index, partner])[:, None] * per_quad + jnp.arange(per_quad)[None, :]
    phase = theta_of(sources)[:, :, None, None] * (moment_of.astype(F32) + 1.0)[None, None]
    cos, sin = jnp.cos(phase) / quads_total, jnp.sin(phase) / quads_total
    coef = jnp.stack(
        [jnp.stack([cos, sin], axis=-1), jnp.stack([-sin, cos], axis=-1)], axis=2
    )
    send_mix = jnp.einsum("rqptak,lm->trqplakm", coef[:, :, :, 1:], jnp.eye(h, dtype=F32))
    send_mix = send_mix.reshape(pairs - 1, 2 * wide, per_device * 2 * h)
    place = jnp.stack([jnp.eye(half, dtype=F32)[c * h : (c + 1) * h] for c in range(CHUNKS)])
    keep_mix = jnp.einsum("rqpak,clm->crqplakm", coef[:, :, :, 0], place)
    keep_mix = keep_mix.reshape(CHUNKS, 2 * wide, per_device * width)
    both_eye = jnp.eye(per_device * 2, dtype=F32).reshape(per_device, 2, per_device, 2)
    place_mix = jnp.einsum("apbk,clm->caplbkm", both_eye, place)
    place_mix = place_mix.reshape(CHUNKS, per_device * 2 * h, per_device * width).astype(BF16)
    send_mix = jnp.swapaxes(split_two(send_mix), 0, 1)
    keep_mix = jnp.swapaxes(split_two(keep_mix), 0, 1)

    rhs_full = rhs.reshape(nb, bs, width)
    rhs_parts = rhs.reshape(rows, 2, CHUNKS, h)
    up = [(i, i + 1) for i in range(row_count - 1)]
    down = [(i + 1, i) for i in range(row_count - 1)]
    swaps = [(i, i + 1 - 2 * (i % 2)) for i in range(quad_count)]

    grid = (nb // tile,)
    pre_spec = pl.BlockSpec((per_quad, tile, bs, 2 * bs), lambda i, *_: (0, i, 0, 0))
    field_spec = pl.BlockSpec((tile, bs, wide), lambda i, *_: (i, 0, 0))
    any_spec = pl.BlockSpec(memory_space=pl.ANY)
    field = jax.ShapeDtypeStruct((nb, bs, wide), BF16)

    def initial(chunk_rhs):
        return pl.pallas_call(
            functools.partial(init_kernel, h),
            grid=grid,
            in_specs=[pre_spec, field_spec],
            out_specs=field_spec,
            out_shape=field,
            compiler_params=params,
            cost_estimate=pl.CostEstimate(
                flops=4 * rows * bs * wide * per_quad, bytes_accessed=4 * rows * wide + 2 * precond.size,
                transcendentals=0,
            ),
            name="initial",
        )(precond, chunk_rhs)

    def sweep(chunk_rhs, before, own, after, last):
        out_specs, out_shape = field_spec, field
        if last:
            out_specs = [field_spec, pl.BlockSpec((width, wide), lambda i, *_: (0, 0))]
            out_shape = [field, jax.ShapeDtypeStruct((width, wide), F32)]
        return pl.pallas_call(
            functools.partial(sweep_kernel, h, last),
            grid_spec=pltpu.PrefetchScalarGridSpec(
                num_scalar_prefetch=1,
                grid=grid,
                in_specs=[
                    pl.BlockSpec((tile, bs, slots * bs), lambda i, *_: (i, 0, 0)),
                    pre_spec,
                    field_spec,
                    pl.BlockSpec((tile, bs, width), lambda i, *_: (i, 0, 0)),
                    pl.BlockSpec((8, wide), lambda i, *_: (0, 0)),
                    any_spec,
                    any_spec,
                    any_spec,
                ],
                out_specs=out_specs,
                scratch_shapes=[
                    pltpu.VMEM((3 * nb + 1, bs, wide), BF16),
                    pltpu.SemaphoreType.DMA((3,)),
                ],
            ),
            out_shape=out_shape,
            compiler_params=params,
            cost_estimate=pl.CostEstimate(
                flops=2 * hamiltonian.size * wide, bytes_accessed=2 * hamiltonian.size + 10 * rows * wide,
                transcendentals=0,
            ),
            name="sweep",
        )(index, hamiltonian, precond, chunk_rhs, rhs_full, coefs, before, own, after)

    tall = 512
    flat_spec = pl.BlockSpec((tall, wide), lambda i: (i, 0))
    sent_spec = pl.BlockSpec((tall, per_device * 2 * h), lambda i: (i, 0))

    def whole_spec(array):
        return pl.BlockSpec(array.shape, lambda i: (0,) * array.ndim)

    def mixed(own, pair, mix):
        return pl.pallas_call(
            mix_kernel,
            grid=(rows // tall,),
            in_specs=[flat_spec, flat_spec, whole_spec(mix)],
            out_specs=sent_spec,
            out_shape=jax.ShapeDtypeStruct((rows, per_device * 2 * h), BF16),
            compiler_params=params,
            cost_estimate=pl.CostEstimate(
                flops=4 * rows * mix.shape[1] * mix.shape[2], bytes_accessed=6 * rows * wide, transcendentals=0
            ),
            name="mixed",
        )(own, pair, mix)

    parts = [
        jnp.concatenate([rhs_parts[:, p, c] for _ in range(per_quad) for p in range(2)], axis=1)
        .reshape(nb, bs, wide)
        for c in range(CHUNKS)
    ]
    finals, partners, received, terms = [], [], [], []
    for c in range(CHUNKS):
        iterate = initial(parts[c])
        term = None
        for sweep_no in range(ITERS):
            before = lax.ppermute(iterate, "row", up)
            after = lax.ppermute(iterate, "row", down)
            last = sweep_no == ITERS - 1
            iterate = sweep(parts[c], before, iterate, after, last)
            if last:
                iterate, term = iterate
        own = iterate.reshape(rows, wide)
        pair = lax.ppermute(own, "quad", swaps)
        finals.append(own)
        partners.append(pair)
        terms.append(term.reshape(width, per_quad, 2, h))
        for d in range(1, pairs):
            route = [
                (p * 2 + s, ((p + d) % pairs) * 2 + 1 - s) for p in range(pairs) for s in range(2)
            ]
            received.append(lax.ppermute(mixed(own, pair, send_mix[d - 1]), "quad", route))

    scale = 1.0 / math.sqrt(rows * row_count)
    orders = jnp.arange(MOMENTS).astype(F32) + 1.0
    terms = jnp.stack(terms, axis=3).reshape(width, per_quad, 2, half)
    own_phase = orders[:, None] * theta_of(points)[None, :]
    own_cos = (jnp.cos(own_phase) * (scale / quads_total))[:, None, :, None]
    own_sin = (jnp.sin(own_phase) * (scale / quads_total))[:, None, :, None]
    re, im = terms[None, :, :, 0], terms[None, :, :, 1]
    block_re = jnp.sum(own_cos * re - own_sin * im, axis=2)
    block_im = jnp.sum(own_cos * im + own_sin * re, axis=2)
    local_blocks = jnp.concatenate([block_re, block_im], axis=-1).astype(BF16)
    all_blocks = lax.psum(local_blocks, ("quad", "row"))
    blocks_out = lax.dynamic_slice_in_dim(all_blocks, quad_index * per_device, per_device, 0).astype(F32)

    moments_out = pl.pallas_call(
        functools.partial(final_kernel, CHUNKS, pairs - 1, per_device),
        grid=(rows // tall,),
        in_specs=[flat_spec] * (2 * CHUNKS)
        + [sent_spec] * len(received)
        + [whole_spec(keep_mix), whole_spec(place_mix)],
        out_specs=pl.BlockSpec((per_device, tall, width), lambda i: (0, i, 0)),
        out_shape=jax.ShapeDtypeStruct((per_device, rows, width), F32),
        compiler_params=params,
        name="final",
    )(*finals, *partners, *received, keep_mix, place_mix)
    return (moments_out, blocks_out)


def solution(mesh):
    return jax.shard_map(
        shards,
        mesh=mesh,
        in_specs=(
            P("row", None, None),
            P("row", None),
            P("row"),
            P("quad", "row", None, None),
            P("row", None),
        ),
        out_specs=(P("quad", "row", None), P("quad", None, None)),
        check_vma=False,
    )
```

```python
import functools
import math

import jax
import jax.numpy as jnp
from jax import lax
from jax.experimental import pallas as pl
from jax.experimental.pallas import tpu as pltpu
from jax.sharding import PartitionSpec as P

ITERS = 2
MOMENTS = 8
CHUNKS = 2
TILE = 16
VMEM_LIMIT = 48 * 1024 * 1024
MESH = pl.DeviceIdType.MESH
F32 = jnp.float32
BF16 = jnp.bfloat16


def rotated(values, h):
    width = values.shape[1]
    lane = lax.broadcasted_iota(jnp.int32, values.shape, 1)
    first = (lane // h) % 2 == 0
    ahead = pltpu.roll(values, width - h, 1)
    behind = pltpu.roll(values, h, 1)
    return jnp.where(first, -ahead, behind)


def apply_inverse(pre_ref, resid, h):
    per_quad, tile = pre_ref.shape[0], pre_ref.shape[1]
    _, bs, width = resid.shape
    turned = rotated(resid.reshape(tile * bs, width), h).astype(BF16)
    plain = resid.astype(BF16).reshape(tile * bs, width)
    lane = lax.broadcasted_iota(jnp.int32, (bs, width), 1)
    outs = []
    for t in range(tile):
        own = slice(t * bs, (t + 1) * bs)
        stacked = jnp.concatenate([plain[own], turned[own]], axis=0)
        blocks = jnp.concatenate([pre_ref[q, t] for q in range(per_quad)], axis=0)
        both = jnp.dot(blocks, stacked, preferred_element_type=F32)
        out = both[:bs]
        for q in range(1, per_quad):
            out = jnp.where(lane // (2 * h) == q, both[q * bs : (q + 1) * bs], out)
        outs.append(out)
    return outs


def init_kernel(h, pre_ref, rhs_ref, out_ref):
    for t, block in enumerate(apply_inverse(pre_ref, rhs_ref[...].astype(F32), h)):
        out_ref[t] = block.astype(BF16)


def sweep_kernel(
    h, last, index_ref, ham_ref, pre_ref, rhs_ref, full_ref, coef_ref, before_ref, own_ref, after_ref, *rest
):
    if last:
        out_ref, terms_ref, held, product, sems = rest
    else:
        out_ref, held, product, sems = rest
    tile, bs, width = out_ref.shape
    nb = own_ref.shape[0]
    slots = ham_ref.shape[2] // bs
    step = pl.program_id(0)

    @pl.when(step == 0)
    def _():
        copies = [
            pltpu.make_async_copy(src, held.at[pl.ds(k * nb, nb)], sems.at[k])
            for k, src in enumerate((before_ref, own_ref, after_ref))
        ]
        for copy in copies:
            copy.start()
        held[3 * nb] = jnp.zeros((bs, width), BF16)
        if last:
            terms_ref[...] = jnp.zeros_like(terms_ref)
        for copy in copies:
            copy.wait()

    zreal = coef_ref[0:1, :]
    zimag = coef_ref[1:2, :]
    for t in range(tile):
        b = step * tile + t
        gathered = jnp.concatenate([held[index_ref[b, s]] for s in range(slots)], axis=0)
        product[t] = jnp.dot(ham_ref[t], gathered, preferred_element_type=F32)
    current = held[pl.ds(nb + step * tile, tile)].astype(F32).reshape(tile * bs, width)
    shifted = zreal * current + zimag * rotated(current, h)
    target = rhs_ref[...].astype(F32).reshape(tile * bs, width)
    resid = (target - (shifted - product[...].reshape(tile * bs, width))).astype(BF16)
    resid = resid.astype(F32).reshape(tile, bs, width)
    for t, block in enumerate(apply_inverse(pre_ref, resid, h)):
        out_ref[t] = (current[t * bs : (t + 1) * bs] + block).astype(BF16)
    if last:
        terms_ref[...] += lax.dot_general(
            full_ref[...].reshape(tile * bs, full_ref.shape[2]),
            out_ref[...].reshape(tile * bs, width),
            (((0,), (0,)), ((), ())),
            preferred_element_type=F32,
        )


def mix_kernel(own_ref, pair_ref, mix_ref, out_ref):
    pack = jnp.concatenate([own_ref[...], pair_ref[...]], axis=1)
    wide = jnp.dot(pack, mix_ref[0], preferred_element_type=F32)
    out_ref[...] = (wide + jnp.dot(pack, mix_ref[1], preferred_element_type=F32)).astype(BF16)


def final_kernel(chunks, others, per_device, *refs):
    own, pair = refs[:chunks], refs[chunks : 2 * chunks]
    got = refs[2 * chunks : (2 + others) * chunks]
    mix_ref, place_ref, out_ref = refs[(2 + others) * chunks :]
    total = None
    for c in range(chunks):
        pack = jnp.concatenate([own[c][...], pair[c][...]], axis=1)
        part = jnp.dot(pack, mix_ref[c, 0], preferred_element_type=F32)
        part = part + jnp.dot(pack, mix_ref[c, 1], preferred_element_type=F32)
        for k in range(others):
            part = part + jnp.dot(
                got[c * others + k][...], place_ref[c], preferred_element_type=F32
            )
        total = part if total is None else total + part
    width = total.shape[1] // per_device
    for a in range(per_device):
        out_ref[a] = total[:, a * width : (a + 1) * width]


def sum_kernel(rows_n, quads_n, coef_ref, terms_ref, out_ref, parts, mine, quads, held, *sems):
    me_row, me_quad = lax.axis_index("row"), lax.axis_index("quad")
    piece = mine.shape[0]
    per_device, width = held.shape[0], held.shape[2]
    per_quad = mine.shape[1] // width
    row_peers = [lax.rem(me_row + d, rows_n) for d in range(1, rows_n)]
    quad_peers = [lax.rem(me_quad + d, quads_n) for d in range(1, quads_n)]

    barrier = pltpu.get_barrier_semaphore()
    for peer in row_peers:
        pl.semaphore_signal(barrier, inc=1, device_id=(me_quad, peer), device_id_type=MESH)
    for peer in quad_peers:
        pl.semaphore_signal(barrier, inc=1, device_id=(peer, me_row), device_id_type=MESH)
    pl.semaphore_wait(barrier, rows_n - 1 + quads_n - 1)

    def send(k, src, dst, peer_quad, peer_row, d):
        copy = pltpu.make_async_remote_copy(
            src_ref=src,
            dst_ref=dst,
            send_sem=sems[2 * k].at[d],
            recv_sem=sems[2 * k + 1].at[d],
            device_id=(peer_quad, peer_row),
            device_id_type=MESH,
        )
        copy.start()
        return copy

    copies = [
        send(0, terms_ref.at[pl.ds(pl.multiple_of(peer * piece, piece), piece)], parts.at[d], me_quad, peer, d)
        for d, peer in enumerate(row_peers)
    ]
    total = terms_ref[pl.ds(pl.multiple_of(me_row * piece, piece), piece), :]
    for d, copy in enumerate(copies):
        copy.wait()
        total = total + parts[d]
    mine[...] = total

    copies = [send(1, mine, quads.at[d], peer, me_row, d) for d, peer in enumerate(quad_peers)]
    sums = [jnp.zeros((piece, width), F32) for _ in range(per_device)]
    for d in range(quads_n):
        if d:
            copies[d - 1].wait()
        for q in range(per_quad):
            part = mine if d == 0 else quads.at[d - 1]
            value = part[:, q * width : (q + 1) * width]
            turned = rotated(value, width // 2)
            for a in range(per_device):
                at = (d * per_quad + q) * per_device + a
                sums[a] = sums[a] + coef_ref[0, at] * value + coef_ref[1, at] * turned
    here = pl.ds(pl.multiple_of(me_row * piece, piece), piece)
    for a in range(per_device):
        held[a, here, :] = sums[a]
    copies = [
        send(2, held.at[:, here], held.at[:, here], me_quad, peer, d) for d, peer in enumerate(row_peers)
    ]
    for copy in copies:
        copy.wait()
    out_ref[...] = held[...]


def split_two(values):
    high = values.astype(BF16)
    low = (values - high.astype(F32)).astype(BF16)
    return jnp.stack([high, low])


def shards(hamiltonian, columns, counts, precond, rhs):
    nb, bs, _ = hamiltonian.shape
    slots = columns.shape[1]
    width = rhs.shape[1]
    half = width // 2
    per_quad = precond.shape[0]
    quad_count = lax.axis_size("quad")
    row_count = lax.axis_size("row")
    quads_total = per_quad * quad_count
    per_device = MOMENTS // quad_count
    rows = nb * bs
    row_index = lax.axis_index("row")
    quad_index = lax.axis_index("quad")
    h = half // CHUNKS
    wide = per_quad * 2 * h
    tile = TILE
    params = pltpu.CompilerParams(vmem_limit_bytes=VMEM_LIMIT)

    first_block = (row_index - 1) * nb
    live = jnp.arange(slots)[None, :] < counts[:, None]
    index = jnp.where(live, columns - first_block, 3 * nb).astype(jnp.int32)

    def theta_of(j):
        return 2.0 * jnp.pi * (j.astype(F32) + 0.5) / quads_total

    points = quad_index * per_quad + jnp.arange(per_quad)
    lane_theta = jnp.repeat(theta_of(points), 2 * h)
    coefs = jnp.concatenate(
        [jnp.cos(lane_theta)[None], jnp.sin(lane_theta)[None], jnp.zeros((6, wide), F32)], axis=0
    )

    partner = quad_index + 1 - 2 * (quad_index % 2)
    pairs = quad_count // 2
    my_pair, my_side = quad_index // 2, quad_index % 2
    owners = [quad_index] + [
        ((my_pair + d) % pairs) * 2 + (1 - my_side) for d in range(1, pairs)
    ]
    moment_of = jnp.stack(owners)[:, None] * per_device + jnp.arange(per_device)[None, :]
    sources = jnp.stack([quad_index, partner])[:, None] * per_quad + jnp.arange(per_quad)[None, :]
    phase = theta_of(sources)[:, :, None, None] * (moment_of.astype(F32) + 1.0)[None, None]
    cos, sin = jnp.cos(phase) / quads_total, jnp.sin(phase) / quads_total
    coef = jnp.stack(
        [jnp.stack([cos, sin], axis=-1), jnp.stack([-sin, cos], axis=-1)], axis=2
    )
    send_mix = jnp.einsum("rqptak,lm->trqplakm", coef[:, :, :, 1:], jnp.eye(h, dtype=F32))
    send_mix = send_mix.reshape(pairs - 1, 2 * wide, per_device * 2 * h)
    place = jnp.stack([jnp.eye(half, dtype=F32)[c * h : (c + 1) * h] for c in range(CHUNKS)])
    keep_mix = jnp.einsum("rqpak,clm->crqplakm", coef[:, :, :, 0], place)
    keep_mix = keep_mix.reshape(CHUNKS, 2 * wide, per_device * width)
    both_eye = jnp.eye(per_device * 2, dtype=F32).reshape(per_device, 2, per_device, 2)
    place_mix = jnp.einsum("apbk,clm->caplbkm", both_eye, place)
    place_mix = place_mix.reshape(CHUNKS, per_device * 2 * h, per_device * width).astype(BF16)
    send_mix = jnp.swapaxes(split_two(send_mix), 0, 1)
    keep_mix = jnp.swapaxes(split_two(keep_mix), 0, 1)

    rhs_full = rhs.reshape(nb, bs, width)
    rhs_parts = rhs.reshape(rows, 2, CHUNKS, h)
    up = [(i, i + 1) for i in range(row_count - 1)]
    down = [(i + 1, i) for i in range(row_count - 1)]
    swaps = [(i, i + 1 - 2 * (i % 2)) for i in range(quad_count)]

    grid = (nb // tile,)
    pre_spec = pl.BlockSpec((per_quad, tile, bs, 2 * bs), lambda i, *_: (0, i, 0, 0))
    field_spec = pl.BlockSpec((tile, bs, wide), lambda i, *_: (i, 0, 0))
    any_spec = pl.BlockSpec(memory_space=pl.ANY)
    field = jax.ShapeDtypeStruct((nb, bs, wide), BF16)

    def initial(chunk_rhs):
        return pl.pallas_call(
            functools.partial(init_kernel, h),
            grid=grid,
            in_specs=[pre_spec, field_spec],
            out_specs=field_spec,
            out_shape=field,
            compiler_params=params,
            cost_estimate=pl.CostEstimate(
                flops=4 * rows * bs * wide * per_quad, bytes_accessed=4 * rows * wide + 2 * precond.size,
                transcendentals=0,
            ),
            name="initial",
        )(precond, chunk_rhs)

    def sweep(chunk_rhs, before, own, after, last):
        out_specs, out_shape = field_spec, field
        if last:
            out_specs = [field_spec, pl.BlockSpec((width, wide), lambda i, *_: (0, 0))]
            out_shape = [field, jax.ShapeDtypeStruct((width, wide), F32)]
        return pl.pallas_call(
            functools.partial(sweep_kernel, h, last),
            grid_spec=pltpu.PrefetchScalarGridSpec(
                num_scalar_prefetch=1,
                grid=grid,
                in_specs=[
                    pl.BlockSpec((tile, bs, slots * bs), lambda i, *_: (i, 0, 0)),
                    pre_spec,
                    field_spec,
                    pl.BlockSpec((tile, bs, width), lambda i, *_: (i, 0, 0)),
                    pl.BlockSpec((8, wide), lambda i, *_: (0, 0)),
                    any_spec,
                    any_spec,
                    any_spec,
                ],
                out_specs=out_specs,
                scratch_shapes=[
                    pltpu.VMEM((3 * nb + 1, bs, wide), BF16),
                    pltpu.VMEM((tile, bs, wide), F32),
                    pltpu.SemaphoreType.DMA((3,)),
                ],
            ),
            out_shape=out_shape,
            compiler_params=params,
            cost_estimate=pl.CostEstimate(
                flops=2 * hamiltonian.size * wide, bytes_accessed=2 * hamiltonian.size + 10 * rows * wide,
                transcendentals=0,
            ),
            name="sweep",
        )(index, hamiltonian, precond, chunk_rhs, rhs_full, coefs, before, own, after)

    tall = 512
    flat_spec = pl.BlockSpec((tall, wide), lambda i: (i, 0))
    sent_spec = pl.BlockSpec((tall, per_device * 2 * h), lambda i: (i, 0))

    def whole_spec(array):
        return pl.BlockSpec(array.shape, lambda i: (0,) * array.ndim)

    def mixed(own, pair, mix):
        return pl.pallas_call(
            mix_kernel,
            grid=(rows // tall,),
            in_specs=[flat_spec, flat_spec, whole_spec(mix)],
            out_specs=sent_spec,
            out_shape=jax.ShapeDtypeStruct((rows, per_device * 2 * h), BF16),
            compiler_params=params,
            cost_estimate=pl.CostEstimate(
                flops=4 * rows * mix.shape[1] * mix.shape[2], bytes_accessed=6 * rows * wide, transcendentals=0
            ),
            name="mixed",
        )(own, pair, mix)

    parts = [
        jnp.concatenate([rhs_parts[:, p, c] for _ in range(per_quad) for p in range(2)], axis=1)
        .reshape(nb, bs, wide)
        for c in range(CHUNKS)
    ]
    finals, partners, received, terms = [], [], [], []
    for c in range(CHUNKS):
        iterate = initial(parts[c])
        term = None
        for sweep_no in range(ITERS):
            before = lax.ppermute(iterate, "row", up)
            after = lax.ppermute(iterate, "row", down)
            last = sweep_no == ITERS - 1
            iterate = sweep(parts[c], before, iterate, after, last)
            if last:
                iterate, term = iterate
        own = iterate.reshape(rows, wide)
        pair = lax.ppermute(own, "quad", swaps)
        finals.append(own)
        partners.append(pair)
        terms.append(term.reshape(width, per_quad, 2, h))
        for d in range(1, pairs):
            route = [
                (p * 2 + s, ((p + d) % pairs) * 2 + 1 - s) for p in range(pairs) for s in range(2)
            ]
            received.append(lax.ppermute(mixed(own, pair, send_mix[d - 1]), "quad", route))

    scale = 1.0 / math.sqrt(rows * row_count)
    terms = jnp.stack(terms, axis=3).reshape(width, per_quad * width)
    order = (quad_index + quad_count - jnp.arange(quad_count)) % quad_count
    seen = order[:, None, None] * per_quad + jnp.arange(per_quad)[None, :, None]
    moment = quad_index * per_device + jnp.arange(per_device)[None, None, :]
    angle = (theta_of(seen) * (moment.astype(F32) + 1.0)).reshape(-1)
    sum_coef = jnp.stack([jnp.cos(angle), jnp.sin(angle)]) * (scale / quads_total)
    piece = width // row_count
    blocks_out = pl.pallas_call(
        functools.partial(sum_kernel, row_count, quad_count),
        in_specs=[pl.BlockSpec(memory_space=pltpu.SMEM), pl.BlockSpec(memory_space=pltpu.VMEM)],
        out_specs=pl.BlockSpec(memory_space=pltpu.VMEM),
        out_shape=jax.ShapeDtypeStruct((per_device, width, width), F32),
        scratch_shapes=[
            pltpu.VMEM((row_count - 1, piece, per_quad * width), F32),
            pltpu.VMEM((piece, per_quad * width), F32),
            pltpu.VMEM((quad_count - 1, piece, per_quad * width), F32),
            pltpu.VMEM((per_device, width, width), F32),
        ]
        + [pltpu.SemaphoreType.DMA((row_count - 1,))] * 2
        + [pltpu.SemaphoreType.DMA((quad_count - 1,))] * 2
        + [pltpu.SemaphoreType.DMA((row_count - 1,))] * 2,
        compiler_params=pltpu.CompilerParams(
            collective_id=0, has_side_effects=True, vmem_limit_bytes=VMEM_LIMIT
        ),
        cost_estimate=pl.CostEstimate(flops=0, bytes_accessed=40 * 1024 * 1024, transcendentals=0),
        name="sum_blocks",
    )(sum_coef, terms)

    moments_out = pl.pallas_call(
        functools.partial(final_kernel, CHUNKS, pairs - 1, per_device),
        grid=(rows // tall,),
        in_specs=[flat_spec] * (2 * CHUNKS)
        + [sent_spec] * len(received)
        + [whole_spec(keep_mix), whole_spec(place_mix)],
        out_specs=pl.BlockSpec((per_device, tall, width), lambda i: (0, i, 0)),
        out_shape=jax.ShapeDtypeStruct((per_device, rows, width), F32),
        compiler_params=params,
        name="final",
    )(*finals, *partners, *received, keep_mix, place_mix)
    return (moments_out, blocks_out)


def solution(mesh):
    return jax.shard_map(
        shards,
        mesh=mesh,
        in_specs=(
            P("row", None, None),
            P("row", None),
            P("row"),
            P("quad", "row", None, None),
            P("row", None),
        ),
        out_specs=(P("quad", "row", None), P("quad", None, None)),
        check_vma=False,
    )
```
